32 devices in a mesh: groups: 2 (over y), tp: 16 (over z, x, core).
Axes of the slice: x: 2, y: 2, z: 4, core: 2. Of those that a mesh axis runs over, the one named last changes fastest.
Arguments:
- cached_block_pool: bfloat16 [2048, 8192], P(('groups', 'tp')), parts along dimension 0
- prefix_block_indices: int32 [256], P('groups'), parts along dimension 0, may hold values from 0 to 255, as said below
- trailing_new_rows: bfloat16 [512, 8192], P(('groups', 'tp')), parts along dimension 0
- input_norm_gain: bfloat16 [8192], replicated, may hold values from 0.099609375 to 1.8984375
- gate_projection_matrix: bfloat16 [28672, 8192], P('tp'), may hold values from -0.0625 to 0.0625
- up_projection_matrix: bfloat16 [28672, 8192], P('tp'), may hold values from -0.0625 to 0.0625
- down_projection_matrix: bfloat16 [28672, 8192], P('tp'), may hold values from -0.03125 to 0.03125
- gate_adapter_first: bfloat16 [8192, 16], replicated, may hold values from -0.0625 to 0.0625
- gate_adapter_second: bfloat16 [16, 28672], P(None, 'tp'), may hold values from -0.75 to 0.75
- up_adapter_first: bfloat16 [8192, 16], replicated, may hold values from -0.0625 to 0.0625
- up_adapter_second: bfloat16 [16, 28672], P(None, 'tp'), may hold values from -0.75 to 0.75
- down_adapter_first: bfloat16 [28672, 16], P('tp'), may hold values from -0.03125 to 0.03125
- down_adapter_second: bfloat16 [16, 8192], replicated, may hold values from -0.75 to 0.75
- output_cotangent_rows: bfloat16 [1536, 8192], P(('groups', 'tp')), parts along dimension 0, may hold values from -0.119628906 to 0.119628906
Outputs:
- gradient_gate_first: float32 [16384, 16], P(('groups', 'tp')), parts along dimension 0
- gradient_gate_second: float32 [16, 57344], P(None, ('groups', 'tp')), parts along dimension 1
- gradient_up_first: float32 [16384, 16], P(('groups', 'tp')), parts along dimension 0
- gradient_up_second: float32 [16, 57344], P(None, ('groups', 'tp')), parts along dimension 1
- gradient_down_first: float32 [57344, 16], P(('groups', 'tp')), parts along dimension 0
- gradient_down_second: float32 [16, 16384], P(None, ('groups', 'tp')), parts along dimension 1
The draws below stay inside these ranges and needn't reach their ends.
There are 2 independent parts, one for each index of `groups`. The reference program is written for one: setup_inputs(seed, part) draws one part's arguments, and reference() takes and returns one part's arrays. A program takes and returns all parts, laid end to end along the dimension named above; an argument that names none is the same for every part. Nothing has to cross between parts.
Inputs may be any that keep to these rules, and one draw needn't show every extreme that they name: `prefix_block_indices`: at most 8 entries name blocks held by one device of tp, and the blocks of some device are named exactly 8 times; entries may repeat.
All inputs are finite; a program needn't handle non-finite values.
Results may differ from the reference program's by a relative error of at most 0.0069.
Values may be sent and summed in bfloat16 or wider, within the bound.
A program may use at most 256 MiB of HBM per device.

```python
import jax
import jax.numpy as jnp
from jax import lax

MODEL_WIDTH = 8192
HIDDEN_UNITS = 28672
ADAPTER_RANK = 16
BLOCK = 4
PREFIX_BLOCKS = 128
SUFFIX = 256
SLOTS = 16
CAP = 8
POOL = 256
TOKENS = 768
N_TP = 16


def draw_prefix_block_indices(key, part):
    key = jax.random.fold_in(key, 11)
    first_key, second_key, third_key = jax.random.split(key, 3)
    total = N_TP * CAP
    owners = jnp.arange(total, dtype=jnp.int32) % N_TP
    shuffled = jax.random.permutation(first_key, total).astype(jnp.int32)
    priority = jnp.where(owners == 0, 0, jnp.where(owners == N_TP - 1, 1, 2)).astype(jnp.int32)
    scores = priority * total + shuffled
    ordering = jnp.argsort(scores, stable=True)
    chosen = owners[ordering][:PREFIX_BLOCKS]
    mixing = jax.random.permutation(second_key, PREFIX_BLOCKS)
    chosen = chosen[mixing]
    places = jax.random.randint(third_key, (PREFIX_BLOCKS,), 0, SLOTS).astype(jnp.int32)
    position = jnp.arange(PREFIX_BLOCKS, dtype=jnp.int32)
    first_low = jnp.argmax((chosen == 0).astype(jnp.int32)).astype(jnp.int32)
    first_high = jnp.argmax((chosen == N_TP - 1).astype(jnp.int32)).astype(jnp.int32)
    places = jnp.where(position == first_low, 0, places)
    places = jnp.where(position == first_high, SLOTS - 1, places)
    return (chosen + N_TP * places).astype(jnp.int32)


def draw_cached_block_pool(key, part):
    key = jax.random.fold_in(key, 23)
    base_key, row_key, col_key = jax.random.split(key, 3)
    count = POOL * BLOCK
    row_scale = jnp.exp(jax.random.uniform(row_key, (count, 1), jnp.float32, -1.15, 1.15))
    col_scale = jnp.exp(jax.random.uniform(col_key, (1, MODEL_WIDTH), jnp.float32, -1.15, 1.15))
    base = jax.random.normal(base_key, (count, MODEL_WIDTH), jnp.float32)
    return (base * row_scale * col_scale).astype(jnp.bfloat16)


def draw_trailing_new_rows(key, part):
    key = jax.random.fold_in(key, 37)
    base_key, row_key, col_key = jax.random.split(key, 3)
    row_scale = jnp.exp(jax.random.uniform(row_key, (SUFFIX, 1), jnp.float32, -1.15, 1.15))
    col_scale = jnp.exp(jax.random.uniform(col_key, (1, MODEL_WIDTH), jnp.float32, -1.15, 1.15))
    base = jax.random.normal(base_key, (SUFFIX, MODEL_WIDTH), jnp.float32)
    return (base * row_scale * col_scale).astype(jnp.bfloat16)


def block_levels(own_key, extent, cuts, least, largest):
    gain, own = 1.0, jax.random.fold_in(own_key, 6)
    for dim, shards_of in cuts:
        draws = jnp.exp(jax.random.uniform(jax.random.fold_in(own, dim), (shards_of,), jnp.float32, least / len(cuts), largest / len(cuts)))
        gain = gain * jnp.repeat(draws, extent[dim] // shards_of).reshape([-1 if axis == dim else 1 for axis in range(len(extent))])
    return gain


def normal_values(rng, dims, width, reach, cuts=(), held_as=jnp.bfloat16):
    factor_of = block_levels(rng, dims, cuts, -0.22, 0.18) if cuts else 1.0
    result = jax.random.normal(rng, dims, jnp.float32) * width * factor_of
    return jnp.minimum(jnp.maximum(result, -reach), reach).astype(held_as)


def setup_inputs(seed: int = 0, part: int = 0) -> dict:
    key_of = jax.random.split(jax.random.key(seed), 15)
    part_keys = jax.random.split(jax.random.fold_in(key_of[14], part), 15)
    cached_block_pool = draw_cached_block_pool(jax.random.fold_in(jax.random.fold_in(key_of[14], part), 71), part)
    prefix_block_indices = draw_prefix_block_indices(jax.random.fold_in(jax.random.fold_in(key_of[14], part), 71), part)
    trailing_new_rows = draw_trailing_new_rows(jax.random.fold_in(jax.random.fold_in(key_of[14], part), 71), part)
    input_norm_gain = jnp.clip(1.0 + 0.18 * jax.random.normal(key_of[3], (MODEL_WIDTH,), jnp.float32), 0.099609375, 1.8984375).astype(jnp.bfloat16)
    gate_projection_matrix = normal_values(key_of[4], (HIDDEN_UNITS, MODEL_WIDTH), MODEL_WIDTH ** -0.5, 0.0625, ((0, 16),))
    up_projection_matrix = normal_values(key_of[5], (HIDDEN_UNITS, MODEL_WIDTH), MODEL_WIDTH ** -0.5, 0.0625, ((0, 16),))
    down_projection_matrix = normal_values(key_of[6], (HIDDEN_UNITS, MODEL_WIDTH), HIDDEN_UNITS ** -0.5, 0.03125, ((0, 16),))
    gate_adapter_first = normal_values(key_of[7], (MODEL_WIDTH, ADAPTER_RANK), MODEL_WIDTH ** -0.5, 0.0625)
    gate_adapter_second = normal_values(key_of[8], (ADAPTER_RANK, HIDDEN_UNITS), (4 * ADAPTER_RANK) ** -0.5, 0.75, ((1, 16),))
    up_adapter_first = normal_values(key_of[9], (MODEL_WIDTH, ADAPTER_RANK), MODEL_WIDTH ** -0.5, 0.0625)
    up_adapter_second = normal_values(key_of[10], (ADAPTER_RANK, HIDDEN_UNITS), (4 * ADAPTER_RANK) ** -0.5, 0.75, ((1, 16),))
    down_adapter_first = normal_values(key_of[11], (HIDDEN_UNITS, ADAPTER_RANK), HIDDEN_UNITS ** -0.5, 0.03125, ((0, 16),))
    down_adapter_second = normal_values(key_of[12], (ADAPTER_RANK, MODEL_WIDTH), (4 * ADAPTER_RANK) ** -0.5, 0.75)
    output_cotangent_rows = normal_values(part_keys[13], (TOKENS, MODEL_WIDTH), 0.02, 0.119628906, ((0, 16),))
    return dict(cached_block_pool=cached_block_pool, prefix_block_indices=prefix_block_indices, trailing_new_rows=trailing_new_rows, input_norm_gain=input_norm_gain, gate_projection_matrix=gate_projection_matrix, up_projection_matrix=up_projection_matrix, down_projection_matrix=down_projection_matrix, gate_adapter_first=gate_adapter_first, gate_adapter_second=gate_adapter_second, up_adapter_first=up_adapter_first, up_adapter_second=up_adapter_second, down_adapter_first=down_adapter_first, down_adapter_second=down_adapter_second, output_cotangent_rows=output_cotangent_rows)


ADAPTER_SCALE = 2.0

def narrow_product(left, right):
    return jnp.dot(left.astype(jnp.float32), right.astype(jnp.float32), precision=lax.Precision.HIGHEST)

def reference(cached_block_pool, prefix_block_indices, trailing_new_rows, input_norm_gain, gate_projection_matrix, up_projection_matrix, down_projection_matrix, gate_adapter_first, gate_adapter_second, up_adapter_first, up_adapter_second, down_adapter_first, down_adapter_second, output_cotangent_rows):
    stored = cached_block_pool.reshape(N_TP, SLOTS, BLOCK, MODEL_WIDTH)
    owners = (prefix_block_indices % N_TP).astype(jnp.int32)
    places = (prefix_block_indices // N_TP).astype(jnp.int32)
    prefix = stored[owners, places].reshape(PREFIX_BLOCKS * BLOCK, MODEL_WIDTH)
    rows = jnp.concatenate([prefix, trailing_new_rows], axis=0)
    widened = rows.astype(jnp.float32)
    scale_rows = lax.rsqrt(lax.optimization_barrier(jnp.mean(widened * widened, axis=1, keepdims=True)) + 1e-05)
    normalized_rows = (widened * scale_rows * input_norm_gain.astype(jnp.float32)).astype(jnp.bfloat16)
    gate_rank_product = narrow_product(normalized_rows, gate_adapter_first).astype(jnp.bfloat16)
    up_rank_product = narrow_product(normalized_rows, up_adapter_first).astype(jnp.bfloat16)
    gate_projected_rows = jnp.dot(normalized_rows, gate_projection_matrix.T, preferred_element_type=jnp.float32) + ADAPTER_SCALE * narrow_product(gate_rank_product, gate_adapter_second)
    up_projected_rows = jnp.dot(normalized_rows, up_projection_matrix.T, preferred_element_type=jnp.float32) + ADAPTER_SCALE * narrow_product(up_rank_product, up_adapter_second)
    sigmoid_gate = jax.nn.sigmoid(gate_projected_rows)
    activated = gate_projected_rows * sigmoid_gate
    hidden_activation = (activated * up_projected_rows).astype(jnp.bfloat16)
    down_rank_product = narrow_product(hidden_activation, down_adapter_first)
    gradient_rank_product = narrow_product(output_cotangent_rows, down_adapter_second.T).astype(jnp.bfloat16)
    gradient_hidden_units = jnp.dot(output_cotangent_rows, down_projection_matrix.T, preferred_element_type=jnp.float32) + ADAPTER_SCALE * narrow_product(gradient_rank_product, down_adapter_first.T)
    gradient_gate_rows = (gradient_hidden_units * up_projected_rows * sigmoid_gate * (1.0 + gate_projected_rows * (1.0 - sigmoid_gate))).astype(jnp.bfloat16)
    gradient_up_rows = (gradient_hidden_units * activated).astype(jnp.bfloat16)
    gate_backward_signal = narrow_product(gradient_gate_rows, gate_adapter_second.T)
    up_backward_signal = narrow_product(gradient_up_rows, up_adapter_second.T)
    gradient_gate_second = ADAPTER_SCALE * narrow_product(gate_rank_product.T, gradient_gate_rows)
    gradient_up_second = ADAPTER_SCALE * narrow_product(up_rank_product.T, gradient_up_rows)
    gradient_gate_first = ADAPTER_SCALE * narrow_product(normalized_rows.T, gate_backward_signal)
    gradient_up_first = ADAPTER_SCALE * narrow_product(normalized_rows.T, up_backward_signal)
    gradient_down_first = ADAPTER_SCALE * narrow_product(hidden_activation.T, gradient_rank_product)
    gradient_down_second = ADAPTER_SCALE * narrow_product(down_rank_product.T, output_cotangent_rows)
    return (gradient_gate_first, gradient_gate_second, gradient_up_first, gradient_up_second, gradient_down_first, gradient_down_second)
```

```python
import jax
import jax.numpy as jnp
from jax import lax
from jax.sharding import PartitionSpec as P

BLOCK = 4
ADAPTER_SCALE = 2.0


def narrow(left, right, left_dim, right_dim):
    return lax.dot_general(
        left, right, (((left_dim,), (right_dim,)), ((), ())), preferred_element_type=jnp.float32
    )


def exact(left, right, left_dim, right_dim):
    return lax.dot_general(
        left.astype(jnp.float32),
        right.astype(jnp.float32),
        (((left_dim,), (right_dim,)), ((), ())),
        precision=lax.Precision.HIGHEST,
    )


def own_rows(pool, indices, suffix, gain, devices, my_index):
    count = indices.shape[0]
    capacity = count // devices
    owners = indices % devices
    places = indices // devices
    position = jnp.arange(count)
    before = (owners[:, None] == owners[None, :]) & (position[None, :] < position[:, None])
    ranking = jnp.sum(before.astype(jnp.int32), axis=1)
    picked = (owners[None, :] == my_index) & (ranking[None, :] == jnp.arange(capacity)[:, None])
    slot = jnp.sum(jnp.where(picked, places[None, :], 0), axis=1)
    source = (slot[:, None] * BLOCK + jnp.arange(BLOCK)[None, :]).reshape(-1)
    select = (source[:, None] == jnp.arange(pool.shape[0])[None, :]).astype(jnp.bfloat16)
    packed = narrow(select, pool, 1, 0)
    rows = jnp.concatenate([packed, suffix.astype(jnp.float32)], axis=0)
    scale = lax.rsqrt(jnp.mean(rows * rows, axis=1, keepdims=True) + 1e-05)
    normed = (rows * scale * gain.astype(jnp.float32)).astype(jnp.bfloat16)
    held, new = capacity * BLOCK, suffix.shape[0]
    per = held + new
    prefix_at = owners * per + ranking * BLOCK
    prefix_at = (prefix_at[:, None] + jnp.arange(BLOCK)[None, :]).reshape(-1)
    suffix_at = (jnp.arange(devices)[:, None] * per + held + jnp.arange(new)[None, :]).reshape(-1)
    arrived_at = jnp.concatenate([prefix_at, suffix_at])
    order = (arrived_at[:, None] == jnp.arange(devices * per)[None, :]).astype(jnp.bfloat16)
    return normed, order


def shards(
    cached_block_pool,
    prefix_block_indices,
    trailing_new_rows,
    input_norm_gain,
    gate_projection_matrix,
    up_projection_matrix,
    down_projection_matrix,
    gate_adapter_first,
    gate_adapter_second,
    up_adapter_first,
    up_adapter_second,
    down_adapter_first,
    down_adapter_second,
    output_cotangent_rows,
):
    devices = lax.axis_size("tp")
    my_index = lax.axis_index("tp")
    width = cached_block_pool.shape[1]
    rank = gate_adapter_first.shape[1]
    normed_own, order = own_rows(
        cached_block_pool,
        prefix_block_indices,
        trailing_new_rows,
        input_norm_gain,
        devices,
        my_index,
    )
    arrived = lax.all_gather(normed_own, "tp", axis=0, tiled=True)
    cotangent = lax.all_gather(output_cotangent_rows, "tp", axis=0, tiled=True)
    normed = narrow(order, arrived, 1, 0).astype(jnp.bfloat16)
    both_first = jnp.concatenate([gate_adapter_first, up_adapter_first], axis=1)
    low = narrow(normed, both_first, 1, 0).astype(jnp.bfloat16)
    gate_low, up_low = low[:, :rank], low[:, rank:]
    gate_proj = narrow(normed, gate_projection_matrix, 1, 1) + ADAPTER_SCALE * narrow(
        gate_low, gate_adapter_second, 1, 0
    )
    up_proj = narrow(normed, up_projection_matrix, 1, 1) + ADAPTER_SCALE * narrow(
        up_low, up_adapter_second, 1, 0
    )
    sigmoid = jax.nn.sigmoid(gate_proj)
    activated = gate_proj * sigmoid
    hidden = (activated * up_proj).astype(jnp.bfloat16)
    grad_low = narrow(cotangent, down_adapter_second, 1, 1).astype(jnp.bfloat16)
    grad_hidden = narrow(cotangent, down_projection_matrix, 1, 1) + ADAPTER_SCALE * narrow(
        grad_low, down_adapter_first, 1, 1
    )
    grad_gate = (
        grad_hidden * up_proj * sigmoid * (1.0 + gate_proj * (1.0 - sigmoid))
    ).astype(jnp.bfloat16)
    grad_up = (grad_hidden * activated).astype(jnp.bfloat16)
    partial = jnp.concatenate(
        [
            narrow(hidden, down_adapter_first, 1, 0),
            narrow(grad_gate, gate_adapter_second, 1, 1),
            narrow(grad_up, up_adapter_second, 1, 1),
        ],
        axis=1,
    )
    total = lax.psum(partial, "tp")
    gate_second = ADAPTER_SCALE * narrow(gate_low, grad_gate, 0, 0)
    up_second = ADAPTER_SCALE * narrow(up_low, grad_up, 0, 0)
    down_first = ADAPTER_SCALE * narrow(hidden, grad_low, 0, 0)
    mine = width // devices
    normed_mine = lax.dynamic_slice_in_dim(normed, my_index * mine, mine, 1)
    cotangent_mine = lax.dynamic_slice_in_dim(cotangent, my_index * mine, mine, 1)
    both = ADAPTER_SCALE * exact(normed_mine, total[:, rank:], 0, 0)
    down_second = ADAPTER_SCALE * exact(total[:, :rank], cotangent_mine, 0, 0)
    return both[:, :rank], gate_second, both[:, rank:], up_second, down_first, down_second


def solution(mesh):
    return jax.shard_map(
        shards,
        mesh=mesh,
        in_specs=(
            P(("groups", "tp"), None),
            P("groups"),
            P(("groups", "tp"), None),
            P(),
            P("tp", None),
            P("tp", None),
            P("tp", None),
            P(),
            P(None, "tp"),
            P(),
            P(None, "tp"),
            P("tp", None),
            P(),
            P(("groups", "tp"), None),
        ),
        out_specs=(
            P(("groups", "tp"), None),
            P(None, ("groups", "tp")),
            P(("groups", "tp"), None),
            P(None, ("groups", "tp")),
            P(("groups", "tp"), None),
            P(None, ("groups", "tp")),
        ),
        check_vma=False,
    )
```

```python
import jax
import jax.numpy as jnp
from jax import lax
from jax.experimental import pallas as pl
from jax.experimental.pallas import tpu as pltpu
from jax.sharding import PartitionSpec as P

BLOCK = 4
ADAPTER_SCALE = 2.0


def narrow(left, right, left_dim, right_dim):
    return lax.dot_general(
        left, right, (((left_dim,), (right_dim,)), ((), ())), preferred_element_type=jnp.float32
    )


def exact(left, right, left_dim, right_dim):
    return lax.dot_general(
        left.astype(jnp.float32),
        right.astype(jnp.float32),
        (((left_dim,), (right_dim,)), ((), ())),
        precision=lax.Precision.HIGHEST,
    )


def own_rows(pool, indices, suffix, gain, devices, my_index):
    count = indices.shape[0]
    capacity = count // devices
    owners = indices % devices
    places = indices // devices
    position = jnp.arange(count)
    before = (owners[:, None] == owners[None, :]) & (position[None, :] < position[:, None])
    ranking = jnp.sum(before.astype(jnp.int32), axis=1)
    picked = (owners[None, :] == my_index) & (ranking[None, :] == jnp.arange(capacity)[:, None])
    slot = jnp.sum(jnp.where(picked, places[None, :], 0), axis=1)
    source = (slot[:, None] * BLOCK + jnp.arange(BLOCK)[None, :]).reshape(-1)
    select = (source[:, None] == jnp.arange(pool.shape[0])[None, :]).astype(jnp.bfloat16)
    packed = narrow(select, pool, 1, 0)
    rows = jnp.concatenate([packed, suffix.astype(jnp.float32)], axis=0)
    scale = lax.rsqrt(jnp.mean(rows * rows, axis=1, keepdims=True) + 1e-05)
    normed = (rows * scale * gain.astype(jnp.float32)).astype(jnp.bfloat16)
    held, new = capacity * BLOCK, suffix.shape[0]
    per = held + new
    prefix_at = owners * per + ranking * BLOCK
    prefix_at = (prefix_at[:, None] + jnp.arange(BLOCK)[None, :]).reshape(-1)
    suffix_at = (jnp.arange(devices)[:, None] * per + held + jnp.arange(new)[None, :]).reshape(-1)
    arrived_at = jnp.concatenate([prefix_at, suffix_at])
    order = (arrived_at[:, None] == jnp.arange(devices * per)[None, :]).astype(jnp.bfloat16)
    return normed, order


MESH = pl.DeviceIdType.MESH
TILE = 256
PANEL = 640
CHUNK = 2048
STRIP = 128


def layer_kernel(
    rows_own,
    cotangent_own,
    order,
    gate_w,
    up_w,
    down_w,
    gate_ext,
    down_ext,
    hidden_back,
    gate_back,
    up_back,
    arrived,
    summed_out,
    gate_second,
    up_second,
    down_first,
    rows_mine,
    cotangent_mine,
    rows,
    cotangent,
    weights,
    projected,
    panels,
    total,
    hidden,
    grad_gate,
    grad_up,
    weight_sem,
    panel_sem,
    own_sem,
    send_sem,
    recv_sem,
    partial,
    pieces,
    summed,
    pair_send,
    pair_recv,
):
    me = lax.axis_index("tp")
    z, x, core = me // 4, lax.rem(me // 2, 2), lax.rem(me, 2)
    across = z * 4 + (1 - x) * 2 + core
    sibling = z * 4 + x * 2 + (1 - core)
    wide, width = rows.shape[1], gate_w.shape[1]
    tiles = gate_w.shape[0] // TILE
    depth = rows_own.shape[0]
    row_slots = arrived
    cot_slots = cotangent

    def block_at(slots, block):
        return slots.at[pl.ds(pl.multiple_of(block * depth, depth), depth)]

    def copy_to(which, block, send, target):
        slots = row_slots if which == 0 else cot_slots
        return pltpu.make_async_remote_copy(
            src_ref=block_at(slots, block),
            dst_ref=block_at(slots, block),
            send_sem=send_sem.at[which, send],
            recv_sem=recv_sem.at[which, block],
            device_id={"tp": target},
            device_id_type=MESH,
        )

    def weight_copy(tile, slot):
        first = pl.ds(pl.multiple_of(lax.rem(tile, tiles) * TILE, TILE), TILE)
        return first, weights.at[slot], weight_sem.at[slot]

    def weight_start(tile, slot):
        first, target, sem = weight_copy(tile, slot)

        @pl.when(tile < tiles)
        def _():
            pltpu.make_async_copy(gate_w.at[first], target, sem).start()

        @pl.when((tile >= tiles) & (tile < 2 * tiles))
        def _():
            pltpu.make_async_copy(up_w.at[first], target, sem).start()

        @pl.when((tile >= 2 * tiles) & (tile < 3 * tiles))
        def _():
            pltpu.make_async_copy(down_w.at[first], target, sem).start()

    def weight_wait(slot):
        pltpu.make_async_copy(gate_w.at[pl.ds(0, TILE)], weights.at[slot], weight_sem.at[slot]).wait()

    own_rows_copy = pltpu.make_async_copy(rows_own, block_at(row_slots, me), own_sem.at[0])
    own_cot_copy = pltpu.make_async_copy(cotangent_own, block_at(cot_slots, me), own_sem.at[1])
    own_rows_copy.start()
    own_cot_copy.start()
    weight_start(jnp.int32(0), 0)
    weight_start(jnp.int32(1), 1)

    barrier = pltpu.get_barrier_semaphore()
    for step in range(1, 16):
        pl.semaphore_signal(
            barrier, inc=1, device_id={"tp": lax.rem(me + step, 16)}, device_id_type=MESH
        )
    pl.semaphore_wait(barrier, 15)

    above, below = jnp.minimum(z + 1, 3), jnp.maximum(z - 1, 0)
    above, below = above * 4 + x * 2 + core, below * 4 + x * 2 + core

    def each_source(slot, side, act):
        step = slot // 2 + 1
        source = z - step if slot % 2 == 0 else z + step
        valid = source >= 0 if slot % 2 == 0 else source <= 3
        pl.when(valid)(lambda: act(source, source * 4 + (x if side == 0 else 1 - x) * 2 + core))

    def send_own_column(which):
        pl.when(z < 3)(lambda: copy_to(which, me, 0, above).start())
        pl.when(z > 0)(lambda: copy_to(which, me, 4, below).start())

    def send_across(which):
        copy_to(which, me, 8 + z, across).start()

    def send_sibling(which):
        copy_to(which, me, 12 + z, sibling).start()

    def column_event(which, slot):
        def act(source, block):
            copy_to(which, block, 0, sibling).wait_recv()
            step = slot // 2 + 1
            if slot % 2 == 0 and step < 3:
                pl.when(z < 3)(lambda: copy_to(which, block, step, above).start())
            if slot % 2 == 1 and step < 3:
                pl.when(z > 0)(lambda: copy_to(which, block, 4 + step, below).start())
            copy_to(which, block, 8 + source, across).start()
            copy_to(which, block, 12 + source, sibling).start()

        each_source(slot, 0, act)

    def other_act(which):
        def act(source, block):
            copy_to(which, block, 0, sibling).wait_recv()
            copy_to(which, block, 16 + source, sibling).start()

        return act

    def other_event(which, slot):
        each_source(slot, 1, other_act(which))

    def other_own(which):
        other_act(which)(z, across)

    own_rows_copy.wait()
    own_cot_copy.wait()
    send_own_column(0)
    send_across(0)
    send_sibling(0)
    for slot in range(6):
        column_event(0, slot)
        if slot == 1:
            other_own(0)
        if slot == 3:
            other_event(0, 0)
            other_event(0, 1)
    send_own_column(1)
    send_across(1)
    for slot in (2, 3, 4, 5):
        other_event(0, slot)
    send_sibling(1)

    def last_wait(which):
        for step in range(4):
            for side in (0, 1):
                block = lax.rem(z - step + 4, 4) * 4 + (x if side == 0 else 1 - x) * 2 + (1 - core)
                copy_to(which, block, 0, sibling).wait_recv()

    last_wait(0)

    def panel_copy(index, slot):
        columns = pl.ds(pl.multiple_of(index * PANEL, PANEL), PANEL)
        return pltpu.make_async_copy(arrived.at[:, columns], panels.at[slot], panel_sem.at[slot])

    count = wide // PANEL
    panel_copy(0, 0).start()

    @pl.loop(0, count)
    def _(index):
        slot = lax.rem(index, 2)

        @pl.when(index + 1 < count)
        def _():
            panel_copy(index + 1, 1 - slot).start()

        panel_copy(index, slot).wait()
        columns = pl.ds(pl.multiple_of(index * PANEL, PANEL), PANEL)
        rows[:, columns] = jnp.dot(
            order[...], panels[slot], preferred_element_type=jnp.float32
        ).astype(jnp.bfloat16)

    def product(left, right, left_dim, right_dim):
        return lax.dot_general(
            left, right, (((left_dim,), (right_dim,)), ((), ())), preferred_element_type=jnp.float32
        )

    def project(left, slot, extra, out):
        out[...] = product(left[:, width:], extra, 1, 1)

        @pl.loop(0, width // CHUNK)
        def _(part):
            columns = pl.ds(pl.multiple_of(part * CHUNK, CHUNK), CHUNK)
            out[...] += product(left[:, columns], weights[slot, :, columns], 1, 1)

    @pl.loop(0, 2 * tiles)
    def _(tile):
        slot = lax.rem(tile, 2)

        for at, events in (
            (0, (lambda: column_event(1, 0), lambda: column_event(1, 1))),
            (2, (lambda: column_event(1, 2), lambda: column_event(1, 3))),
            (3, (lambda: other_own(1),)),
            (5, (lambda: column_event(1, 4), lambda: column_event(1, 5))),
            (7, (lambda: other_event(1, 0), lambda: other_event(1, 1))),
            (10, (lambda: other_event(1, 2), lambda: other_event(1, 3))),
        ):

            @pl.when(tile == at)
            def _(events=events):
                for event in events:
                    event()

        weight_wait(slot)
        own = pl.ds(pl.multiple_of(tile * TILE, TILE), TILE)
        project(rows, slot, gate_ext[own, :], projected.at[tile])
        weight_start(tile + 2, slot)

    other_event(1, 4)
    other_event(1, 5)
    last_wait(1)
    low_t = jnp.transpose(rows[:, width:].astype(jnp.float32)).astype(jnp.bfloat16)
    grad_low_t = jnp.transpose(cotangent[:, width:].astype(jnp.float32)).astype(jnp.bfloat16)
    partial[...] = jnp.zeros_like(partial)
    share = pl.ds(pl.multiple_of(me * rows_mine.shape[1], rows_mine.shape[1]), rows_mine.shape[1])
    rows_mine[...] = rows[:, share]
    cotangent_mine[...] = cotangent[:, share]

    @pl.loop(0, tiles)
    def _(tile):
        slot = lax.rem(tile, 2)
        own = pl.ds(pl.multiple_of(tile * TILE, TILE), TILE)
        weight_wait(slot)
        project(cotangent, slot, down_ext[own, :], total)
        weight_start(tile + 2 + 2 * tiles, slot)

        @pl.loop(0, rows.shape[0] // STRIP)
        def _(strip):
            at = pl.ds(pl.multiple_of(strip * STRIP, STRIP), STRIP)
            gate = projected[tile, at, :]
            up = projected[tile + tiles, at, :]
            grad = total[at, :]
            sigmoid = 1.0 / (1.0 + jnp.exp(-gate))
            active = gate * sigmoid
            one = (active * up).astype(jnp.bfloat16)
            two = (grad * up * sigmoid * (1.0 + gate * (1.0 - sigmoid))).astype(jnp.bfloat16)
            three = (grad * active).astype(jnp.bfloat16)
            hidden[at, :] = one
            grad_gate[at, :] = two
            grad_up[at, :] = three
            partial[at, :] += (
                product(one, hidden_back[own, :], 1, 0)
                + product(two, gate_back[own, :], 1, 0)
                + product(three, up_back[own, :], 1, 0)
            )

        gate_second[tile] = product(low_t, grad_gate[...], 1, 0)
        up_second[tile] = product(low_t, grad_up[...], 1, 0)
        down_first[tile] = product(grad_low_t, hidden[...], 1, 0)

    def piece_copy(block, slot, target):
        return pltpu.make_async_remote_copy(
            src_ref=block_at(partial, block),
            dst_ref=pieces.at[slot],
            send_sem=pair_send.at[0, block],
            recv_sem=pair_recv.at[0, slot],
            device_id={"tp": target},
            device_id_type=MESH,
        )

    def sum_copy(block, send, target):
        return pltpu.make_async_remote_copy(
            src_ref=block_at(summed, block),
            dst_ref=block_at(summed, block),
            send_sem=pair_send.at[1, send],
            recv_sem=pair_recv.at[1, block],
            device_id={"tp": target},
            device_id_type=MESH,
        )

    @pl.loop(1, 16)
    def _(step):
        other = lax.rem(me + step, 16)
        piece_copy(other, me, other).start()

    pieces[me] = partial[pl.ds(pl.multiple_of(me * depth, depth), depth), :]

    @pl.loop(1, 16)
    def _(step):
        piece_copy(me, lax.rem(me + step, 16), sibling).wait_recv()

    summed[pl.ds(pl.multiple_of(me * depth, depth), depth), :] = jnp.sum(pieces[...], axis=0)

    @pl.loop(1, 16)
    def _(step):
        other = lax.rem(me + step, 16)
        sum_copy(me, other, other).start()

    @pl.loop(1, 16)
    def _(step):
        sum_copy(lax.rem(me + step, 16), me, sibling).wait_recv()

    summed_out[...] = summed[...]

    @pl.loop(1, 16)
    def _(step):
        other = lax.rem(me + step, 16)
        piece_copy(other, me, sibling).wait_send()
        sum_copy(me, other, sibling).wait_send()

    for which in (0, 1):
        for step in range(3):
            pl.when((z < 3) & (z >= step))(
                lambda: copy_to(which, me, step, sibling).wait_send()
            )
            pl.when((z > 0) & (z + step <= 3))(
                lambda: copy_to(which, me, 4 + step, sibling).wait_send()
            )
        for send in range(8, 20):
            copy_to(which, me, send, sibling).wait_send()


def layer(rows_own, cotangent_own, order, gate_w, up_w, down_w, gate_up_ext, down_ext, backs, mine):
    depth, wide = rows_own.shape
    tokens, units = order.shape[0], gate_w.shape[0]
    tiles = units // TILE
    bf16, f32 = jnp.bfloat16, jnp.float32
    anywhere, vmem = pl.BlockSpec(memory_space=pl.ANY), pl.BlockSpec(memory_space=pltpu.VMEM)
    return pl.pallas_call(
        layer_kernel,
        out_shape=(
            jax.ShapeDtypeStruct((tokens, wide), bf16),
            jax.ShapeDtypeStruct((tokens, 128), f32),
            jax.ShapeDtypeStruct((tiles, 128, TILE), f32),
            jax.ShapeDtypeStruct((tiles, 128, TILE), f32),
            jax.ShapeDtypeStruct((tiles, 128, TILE), f32),
            jax.ShapeDtypeStruct((tokens, mine), bf16),
            jax.ShapeDtypeStruct((tokens, mine), bf16),
        ),
        in_specs=[anywhere, anywhere, vmem, anywhere, anywhere, anywhere] + [vmem] * 5,
        out_specs=(anywhere,) + (vmem,) * 6,
        scratch_shapes=[
            pltpu.VMEM((tokens, wide), bf16),
            pltpu.VMEM((tokens, wide), bf16),
            pltpu.VMEM((2, TILE, wide - 128), bf16),
            pltpu.VMEM((2 * tiles, tokens, TILE), f32),
            pltpu.VMEM((2, tokens, PANEL), bf16),
            pltpu.VMEM((tokens, TILE), f32),
            pltpu.VMEM((tokens, TILE), bf16),
            pltpu.VMEM((tokens, TILE), bf16),
            pltpu.VMEM((tokens, TILE), bf16),
            pltpu.SemaphoreType.DMA((2,)),
            pltpu.SemaphoreType.DMA((2,)),
            pltpu.SemaphoreType.DMA((2,)),
            pltpu.SemaphoreType.DMA((2, 20)),
            pltpu.SemaphoreType.DMA((2, 16)),
            pltpu.VMEM((tokens, 128), f32),
            pltpu.VMEM((16, depth, 128), f32),
            pltpu.VMEM((tokens, 128), f32),
            pltpu.SemaphoreType.DMA((2, 16)),
            pltpu.SemaphoreType.DMA((2, 16)),
        ],
        compiler_params=pltpu.CompilerParams(
            collective_id=0, has_side_effects=True, vmem_limit_bytes=62 * 1024 * 1024
        ),
    )(rows_own, cotangent_own, order, gate_w, up_w, down_w, gate_up_ext, down_ext, *backs)


def at_columns(array, start):
    return jnp.pad(array, ((0, 0), (start, 128 - start - array.shape[1])))


def fused(normed_own, order, devices, my_index, width, rank, arrays):
    gate_w, up_w, down_w, gate_first, gate_s, up_first, up_s, down_f, down_s, cot_own = arrays
    both_first = jnp.concatenate([gate_first, up_first], axis=1)
    low = narrow(normed_own, both_first, 1, 0).astype(jnp.bfloat16)
    grad_low = narrow(cot_own, down_s, 1, 1).astype(jnp.bfloat16)
    gate_t, up_t = gate_s.T, up_s.T
    twice = jnp.bfloat16(ADAPTER_SCALE)
    ext = jnp.concatenate(
        [at_columns(twice * gate_t, 0), at_columns(twice * up_t, rank)], axis=0
    )
    _, total, gate_second, up_second, down_first, rows_mine, cot_mine = layer(
        jnp.concatenate([normed_own, at_columns(low, 0)], axis=1),
        jnp.concatenate([cot_own, at_columns(grad_low, 0)], axis=1),
        order,
        gate_w,
        up_w,
        down_w,
        ext,
        at_columns(twice * down_f, 0),
        (at_columns(down_f, 0), at_columns(gate_t, rank), at_columns(up_t, 2 * rank)),
        width // devices,
    )

    def second(tiled, start):
        cut = ADAPTER_SCALE * tiled[:, start : start + rank, :]
        return cut.transpose(1, 0, 2).reshape(rank, -1)

    both = ADAPTER_SCALE * exact(rows_mine, total[:, rank : 3 * rank], 0, 0)
    down_second = ADAPTER_SCALE * exact(total[:, :rank], cot_mine, 0, 0)
    return (
        both[:, :rank],
        second(gate_second, 0),
        both[:, rank:],
        second(up_second, rank),
        second(down_first, 0).T,
        down_second,
    )


def shards(
    cached_block_pool,
    prefix_block_indices,
    trailing_new_rows,
    input_norm_gain,
    gate_projection_matrix,
    up_projection_matrix,
    down_projection_matrix,
    gate_adapter_first,
    gate_adapter_second,
    up_adapter_first,
    up_adapter_second,
    down_adapter_first,
    down_adapter_second,
    output_cotangent_rows,
):
    devices = lax.axis_size("tp")
    my_index = lax.axis_index("tp")
    width = cached_block_pool.shape[1]
    rank = gate_adapter_first.shape[1]
    normed_own, order = own_rows(
        cached_block_pool,
        prefix_block_indices,
        trailing_new_rows,
        input_norm_gain,
        devices,
        my_index,
    )
    if devices == 16 and normed_own.shape[0] == output_cotangent_rows.shape[0] == 48:
        return fused(
            normed_own,
            order,
            devices,
            my_index,
            width,
            rank,
            (
                gate_projection_matrix,
                up_projection_matrix,
                down_projection_matrix,
                gate_adapter_first,
                gate_adapter_second,
                up_adapter_first,
                up_adapter_second,
                down_adapter_first,
                down_adapter_second,
                output_cotangent_rows,
            ),
        )
    arrived = lax.all_gather(normed_own, "tp", axis=0, tiled=True)
    cotangent = lax.all_gather(output_cotangent_rows, "tp", axis=0, tiled=True)
    normed = narrow(order, arrived, 1, 0).astype(jnp.bfloat16)
    both_first = jnp.concatenate([gate_adapter_first, up_adapter_first], axis=1)
    low = narrow(normed, both_first, 1, 0).astype(jnp.bfloat16)
    gate_low, up_low = low[:, :rank], low[:, rank:]
    gate_proj = narrow(normed, gate_projection_matrix, 1, 1) + ADAPTER_SCALE * narrow(
        gate_low, gate_adapter_second, 1, 0
    )
    up_proj = narrow(normed, up_projection_matrix, 1, 1) + ADAPTER_SCALE * narrow(
        up_low, up_adapter_second, 1, 0
    )
    sigmoid = jax.nn.sigmoid(gate_proj)
    activated = gate_proj * sigmoid
    hidden = (activated * up_proj).astype(jnp.bfloat16)
    grad_low = narrow(cotangent, down_adapter_second, 1, 1).astype(jnp.bfloat16)
    grad_hidden = narrow(cotangent, down_projection_matrix, 1, 1) + ADAPTER_SCALE * narrow(
        grad_low, down_adapter_first, 1, 1
    )
    grad_gate = (
        grad_hidden * up_proj * sigmoid * (1.0 + gate_proj * (1.0 - sigmoid))
    ).astype(jnp.bfloat16)
    grad_up = (grad_hidden * activated).astype(jnp.bfloat16)
    partial = jnp.concatenate(
        [
            narrow(hidden, down_adapter_first, 1, 0),
            narrow(grad_gate, gate_adapter_second, 1, 1),
            narrow(grad_up, up_adapter_second, 1, 1),
        ],
        axis=1,
    )
    total = lax.psum(partial, "tp")
    gate_second = ADAPTER_SCALE * narrow(gate_low, grad_gate, 0, 0)
    up_second = ADAPTER_SCALE * narrow(up_low, grad_up, 0, 0)
    down_first = ADAPTER_SCALE * narrow(hidden, grad_low, 0, 0)
    mine = width // devices
    normed_mine = lax.dynamic_slice_in_dim(normed, my_index * mine, mine, 1)
    cotangent_mine = lax.dynamic_slice_in_dim(cotangent, my_index * mine, mine, 1)
    both = ADAPTER_SCALE * exact(normed_mine, total[:, rank:], 0, 0)
    down_second = ADAPTER_SCALE * exact(total[:, :rank], cotangent_mine, 0, 0)
    return both[:, :rank], gate_second, both[:, rank:], up_second, down_first, down_second


def solution(mesh):
    return jax.shard_map(
        shards,
        mesh=mesh,
        in_specs=(
            P(("groups", "tp"), None),
            P("groups"),
            P(("groups", "tp"), None),
            P(),
            P("tp", None),
            P("tp", None),
            P("tp", None),
            P(),
            P(None, "tp"),
            P(),
            P(None, "tp"),
            P("tp", None),
            P(),
            P(("groups", "tp"), None),
        ),
        out_specs=(
            P(("groups", "tp"), None),
            P(None, ("groups", "tp")),
            P(("groups", "tp"), None),
            P(None, ("groups", "tp")),
            P(("groups", "tp"), None),
            P(None, ("groups", "tp")),
        ),
        check_vma=False,
    )
```
